512 devices in a mesh: ctx: 16 (over z, core), head: 8 (over y_hi, x), rep: 4 (over y_lo).
Axes of the slice: x: 4, y: 8 (y_hi: 2, y_lo: 4; y = y_hi * 4 + y_lo), z: 8, core: 2. Of those that a mesh axis runs over, the one named last changes fastest.
Arguments:
- queries: bfloat16 [20480, 8192], P(('rep', 'ctx'), 'head'), parts along dimension 0, may hold values from -40 to 40
- keys: bfloat16 [20480, 1024], P(('rep', 'ctx'), 'head'), parts along dimension 0, may hold values from -25 to 25
- values: bfloat16 [20480, 1024], P(('rep', 'ctx'), 'head'), parts along dimension 0, may hold values from -6 to 6
- block_order: int32 [128], P('rep'), parts along dimension 0, may hold values from 0 to 31, each once
Outputs:
- attended: bfloat16 [20480, 8192], P(('rep', 'ctx'), 'head'), parts along dimension 0
The draws below stay inside these ranges and needn't reach their ends.
There are 4 independent parts, one for each index of `rep`. The reference program is written for one: setup_inputs(seed, part) draws one part's arguments, and reference() takes and returns one part's arrays. A program takes and returns all parts, laid end to end along the dimension named above; each array names one. Nothing has to cross between parts.
Inputs may be any that keep to these rules, and one draw needn't show every extreme that they name: A permutation: stored block b, rows b * 160 to (b + 1) * 160 - 1, holds the sequence's block block_order[b].
All inputs are finite; a program needn't handle non-finite values.
Results may differ from the reference program's by a relative error of at most 0.0044.
Values may be sent and summed in bfloat16 or wider, within the bound.
No kernel may reach another device: no remote copies, remote signals or barrier semaphores. Data moves between devices by JAX's collectives and lax.ppermute only.
A program may use at most 64 MiB of HBM per device.

```python
import math
import jax
import jax.numpy as jnp
from jax import lax

QUERY_HEADS = 64
KEY_VALUE_HEADS = 8
HEAD_SIZE = 128
TOK_DEV = 320
SEQUENCE_TOKENS = 5120
NBLK = 32


def shared_keys(key):
    return jnp.clip(jax.random.normal(key, (SEQUENCE_TOKENS, KEY_VALUE_HEADS * HEAD_SIZE), jnp.float32), -6.0, 6.0)


def draw_keys(key, part):
    common_part = shared_keys(key)
    result = common_part
    return result.astype(jnp.bfloat16)


def draw_queries(key, part):
    key = jax.random.fold_in(key, 5)
    own_draw = jnp.clip(jax.random.normal(key, (SEQUENCE_TOKENS, QUERY_HEADS * HEAD_SIZE), jnp.float32), -6.0, 6.0)
    result = own_draw
    return result.astype(jnp.bfloat16)


def shard_levels(key, extent, cuts, least, largest):
    def one(position, blocks):
        heights = jax.random.uniform(jax.random.fold_in(jax.random.fold_in(key, 6), position), (blocks,), jnp.float32, least / len(cuts), largest / len(cuts))
        return jnp.repeat(jnp.exp(heights), extent[position] // blocks).reshape((-1,) + (1,) * (len(extent) - position - 1))

    factor_of = one(*cuts[0])
    for cut in cuts[1:]:
        factor_of = factor_of * one(*cut)
    return factor_of


def centred(rng, shape, deviation, most, pieces=(), held_as=jnp.bfloat16):
    level = shard_levels(rng, shape, pieces, -0.22, 0.18) if pieces else 1.0
    drawn = jax.random.normal(rng, shape, jnp.float32) * deviation * level
    return jnp.minimum(jnp.maximum(drawn, -most), most).astype(held_as)


def setup_inputs(seed: int = 0, part: int = 0) -> dict:
    key_list = jax.random.split(jax.random.key(seed), 5)
    part_keys = jax.random.split(jax.random.fold_in(key_list[4], part), 5)
    queries = draw_queries(jax.random.fold_in(jax.random.fold_in(key_list[4], part), 71), part)
    keys = draw_keys(jax.random.fold_in(jax.random.fold_in(key_list[4], part), 71), part)
    values = centred(part_keys[2], (SEQUENCE_TOKENS, KEY_VALUE_HEADS * HEAD_SIZE), 1.0, 6.0, ((0, 16), (1, 8)))
    block_order = jax.random.permutation(part_keys[3], NBLK).astype(jnp.int32)
    return dict(queries=queries, keys=keys, values=values, block_order=block_order)


NEGATIVE_LIMIT = -1e+30

def block_part(query_rows, query_pos, key_rows, value_rows, key_pos):
    scaling = 1.0 / math.sqrt(query_rows.shape[-1])
    scores = jnp.einsum('rkgd,tkd->rkgt', query_rows, key_rows) * scaling
    visible = (key_pos[None, :] <= query_pos[:, None])[:, None, None, :]
    scores = jnp.where(visible, scores, NEGATIVE_LIMIT)
    maxima = lax.optimization_barrier(jnp.max(scores, axis=-1))
    weights = jnp.where(visible, jnp.exp(scores - maxima[..., None]), 0.0).astype(jnp.bfloat16)
    widened = weights.astype(jnp.float32)
    totals = lax.optimization_barrier(jnp.sum(widened, axis=-1))
    weighted = jnp.einsum('rkgt,tkd->rkgd', widened, value_rows)
    return (maxima, totals, weighted)

def absorb(running, block_result):
    maxima = jnp.maximum(running[0], block_result[0])
    rescale = jnp.exp(running[0] - maxima)
    incoming = jnp.exp(block_result[0] - maxima)
    totals = running[1] * rescale + block_result[1] * incoming
    weighted = running[2] * rescale[..., None] + block_result[2] * incoming[..., None]
    return (maxima, totals, weighted)

def reference(queries, keys, values, block_order):
    count_tokens = queries.shape[0]
    block_rows = TOK_DEV // 2
    group_width = QUERY_HEADS // KEY_VALUE_HEADS
    row_index = jnp.arange(count_tokens, dtype=jnp.int32)
    positions = (block_order[row_index // block_rows] * block_rows + row_index % block_rows).astype(jnp.int32)
    query_full = queries.astype(jnp.float32).reshape(count_tokens, KEY_VALUE_HEADS, group_width, HEAD_SIZE)
    key_full = keys.astype(jnp.float32).reshape(count_tokens, KEY_VALUE_HEADS, HEAD_SIZE)
    value_full = values.astype(jnp.float32).reshape(count_tokens, KEY_VALUE_HEADS, HEAD_SIZE)

    def visit_block(running, block_index):
        first_row = (block_index * block_rows).astype(jnp.int32)
        key_block = lax.dynamic_slice_in_dim(key_full, first_row, block_rows, 0)
        value_block = lax.dynamic_slice_in_dim(value_full, first_row, block_rows, 0)
        pos_block = lax.dynamic_slice_in_dim(positions, first_row, block_rows, 0)
        result = block_part(query_full, positions, key_block, value_block, pos_block)
        return (absorb(running, result), block_index)
    initial_state = (jnp.full((count_tokens, KEY_VALUE_HEADS, group_width), NEGATIVE_LIMIT, jnp.float32), jnp.zeros((count_tokens, KEY_VALUE_HEADS, group_width), jnp.float32), jnp.zeros((count_tokens, KEY_VALUE_HEADS, group_width, HEAD_SIZE), jnp.float32))
    running, spent = lax.scan(visit_block, initial_state, jnp.arange(NBLK, dtype=jnp.int32))
    attended = running[2] / running[1][..., None]
    return attended.astype(jnp.bfloat16).reshape(count_tokens, QUERY_HEADS * HEAD_SIZE)
```

```python
import functools
import math

import jax
import jax.numpy as jnp
from jax import lax
from jax.experimental import pallas as pl
from jax.experimental.pallas import tpu as pltpu
from jax.sharding import PartitionSpec as P

HEAD = 128
GROUP = 8
BLOCK = 160
ROWS = 2 * BLOCK
COLS = GROUP * BLOCK
CHIPS = 8
SUMROWS = HEAD + 16
SCALE = math.log2(math.e) / math.sqrt(HEAD)
NEG = -1e30
LIMIT = 2.0**100
TILES = ((0, 512), (512, 512), (1024, 256))


def dot_nt(a, b):
    return lax.dot_general(a, b, (((1,), (1,)), ((), ())), preferred_element_type=jnp.float32)


def dot_nn(a, b):
    return lax.dot_general(a, b, (((1,), (0,)), ((), ())), preferred_element_type=jnp.float32)


def stage(first, last, offsets, *refs):
    refs = list(refs)
    order_ref, me_ref = refs[:2]
    del refs[:2]
    if first:
        q_ref, own_ref, kv_ref = refs[:3]
        del refs[:3]
    else:
        qs_ref, m_in, acc_in, kv_ref = refs[:4]
        del refs[:4]
    if last:
        o_ref = refs.pop(0)
    elif first:
        qs_ref, m_out, acc_out = refs[:3]
        del refs[:3]
    else:
        m_out, acc_out = refs[:2]
        del refs[:2]
    vt = refs.pop(0)
    if last:
        acc_out, m_out = refs[:2]

    me = me_ref[0]
    z = me // 2
    span = kv_ref.shape[0]
    block_pos = []
    for off in offsets:
        dev = lax.rem(z + (off + CHIPS), CHIPS) * 2
        block_pos += [order_ref[dev * 2 + i] for i in range(4)]

    lane = lax.broadcasted_iota(jnp.int32, (1, span), 1)
    lane_pos = jnp.zeros((1, span), jnp.int32)
    for j, pos in enumerate(block_pos):
        lane_pos = jnp.where((lane >= j * BLOCK) & (lane < (j + 1) * BLOCK), pos, lane_pos)
    values_t = kv_ref[:, HEAD:].astype(jnp.float32).T

    if first:
        for a in range(2):
            key_rows = own_ref[a * BLOCK : (a + 1) * BLOCK, :]
            for h in range(GROUP):
                piece = q_ref[a * BLOCK : (a + 1) * BLOCK, h * HEAD : (h + 1) * HEAD]
                qs_ref[a * COLS + h * BLOCK : a * COLS + (h + 1) * BLOCK, :] = piece
                vt_rows = piece * key_rows
                m_out_rows = a * COLS + h * BLOCK
                refs[-1][m_out_rows : m_out_rows + BLOCK, :] = vt_rows
        for c in range(0, 2 * COLS, 256):
            diag = dot_nt(jnp.ones((8, HEAD), jnp.bfloat16), refs[-1][c : c + 256, :])
            m_out[:, c : c + 256] = diag[:1] * SCALE
        row = lax.broadcasted_iota(jnp.int32, (span, 1), 0)
        key_pos = jnp.zeros((span, 1), jnp.int32)
        for j, pos in enumerate(block_pos):
            key_pos = jnp.where((row >= j * BLOCK) & (row < (j + 1) * BLOCK), pos * BLOCK - j * BLOCK, key_pos)
        key_pos = key_pos + row
        vt[:HEAD, :] = values_t.astype(jnp.bfloat16)
        vt[HEAD:, :] = jnp.ones((SUMROWS - HEAD, span), jnp.bfloat16)

    def visible(a, col, width):
        pos = order_ref[me * 2 + a]
        if first:
            token = lax.rem(lax.broadcasted_iota(jnp.int32, (1, width), 1) + col, BLOCK)
            return key_pos <= token + pos * BLOCK
        return None

    stab = m_out if first else m_in
    over = jnp.zeros((1, 256), jnp.float32)
    for a in range(2):
        q_pos = order_ref[me * 2 + a]
        if not first:
            seen = lane_pos < q_pos
            vt[:HEAD, :] = jnp.where(seen, values_t, 0.0).astype(jnp.bfloat16)
            vt[HEAD:, :] = jnp.broadcast_to(jnp.where(seen, 1.0, 0.0), (SUMROWS - HEAD, span)).astype(jnp.bfloat16)
        for col, width in TILES:
            cols = slice(a * COLS + col, a * COLS + col + width)
            s = dot_nt(kv_ref[:, :HEAD], qs_ref[cols, :])
            p = jnp.exp2(s * SCALE - stab[:, cols])
            if first:
                p = jnp.where(visible(a, col, width), p, 0.0)
            new = dot_nn(vt[...], p.astype(jnp.bfloat16))
            if not first:
                new = new + acc_in[:, cols]
            acc_out[:, cols] = new
            if not first:
                m_out[:, cols] = m_in[:, cols]
            mass = jnp.where(new[HEAD : HEAD + 1] <= LIMIT, 0.0, 1.0)
            for i in range(0, width, 256):
                over = over + mass[:, i : i + 256]

    @pl.when(jnp.sum(over) > 0.0)
    def _():
        def tile(t, carry):
            a = t // (COLS // 256)
            col = (t - a * (COLS // 256)) * 256
            cols = pl.ds(pl.multiple_of(t * 256, 256), 256)
            q_pos = order_ref[me * 2 + a]
            token = lax.rem(lax.broadcasted_iota(jnp.int32, (1, 256), 1) + col, BLOCK) + q_pos * BLOCK
            acc_out[:, cols] = jnp.zeros((SUMROWS, 256), jnp.float32) if first else acc_in[:, cols]
            m_out[:, cols] = stab[:, cols]

            def block(j, carry):
                off = jnp.where(j < 4, offsets[0], offsets[-1])
                pos = order_ref[lax.rem(z + off + CHIPS, CHIPS) * 4 + lax.rem(j, 4)]
                rows = pl.ds(pl.multiple_of(j * BLOCK, BLOCK), BLOCK)
                s = dot_nt(kv_ref[rows, :HEAD], qs_ref[cols, :]) * SCALE
                key = lax.broadcasted_iota(jnp.int32, (BLOCK, 1), 0) + pos * BLOCK
                s = jnp.where(key <= token, s, NEG)
                m = m_out[:, cols]
                peak = jnp.maximum(m, jnp.max(s, axis=0, keepdims=True))
                p = jnp.exp2(s - peak).astype(jnp.bfloat16)
                value = jnp.concatenate(
                    [kv_ref[rows, HEAD:].astype(jnp.float32).T, jnp.ones((SUMROWS - HEAD, BLOCK), jnp.float32)], 0
                )
                acc_out[:, cols] = acc_out[:, cols] * jnp.exp2(m - peak) + dot_nn(value.astype(jnp.bfloat16), p)
                m_out[:, cols] = peak
                return carry

            return lax.fori_loop(0, span // BLOCK, block, carry)

        lax.fori_loop(0, 2 * COLS // 256, tile, 0)

    if last:
        for a in range(2):
            sums = acc_out[:, a * COLS : (a + 1) * COLS]
            full = (sums[:HEAD] * (1.0 / sums[HEAD : HEAD + 1])).T.astype(jnp.bfloat16)
            for h in range(GROUP):
                o_ref[a * BLOCK : (a + 1) * BLOCK, h * HEAD : (h + 1) * HEAD] = full[h * BLOCK : (h + 1) * BLOCK, :]


def run_stage(offsets, scalars, state, kv, last=False):
    first = len(state) == 2
    span = kv.shape[0]
    sums = jax.ShapeDtypeStruct((SUMROWS, 2 * COLS), jnp.float32)
    tops = jax.ShapeDtypeStruct((1, 2 * COLS), jnp.float32)
    rows = jax.ShapeDtypeStruct((2 * COLS, HEAD), jnp.bfloat16)
    scratch = [pltpu.VMEM((SUMROWS, span), jnp.bfloat16)]
    if last:
        out = jax.ShapeDtypeStruct((ROWS, GROUP * HEAD), jnp.bfloat16)
        scratch += [pltpu.VMEM(sums.shape, jnp.float32), pltpu.VMEM(tops.shape, jnp.float32)]
    elif first:
        out = (rows, tops, sums)
        scratch += [pltpu.VMEM(rows.shape, jnp.bfloat16)]
    else:
        out = (tops, sums)
    vmem = pl.BlockSpec(memory_space=pltpu.VMEM)
    smem = pl.BlockSpec(memory_space=pltpu.SMEM)
    pairs = span * 2 * COLS
    result = pl.pallas_call(
        functools.partial(stage, first, last, offsets),
        out_shape=out,
        in_specs=[smem, smem] + [vmem] * (len(state) + 1),
        out_specs=jax.tree.map(lambda _: vmem, out),
        scratch_shapes=scratch,
        compiler_params=pltpu.CompilerParams(vmem_limit_bytes=40 * 2**20),
        cost_estimate=pl.CostEstimate(
            flops=pairs * HEAD * 4, bytes_accessed=span * 512 + 4 * sums.size * 2, transcendentals=pairs
        ),
    )(*scalars, *state, kv)
    if last:
        return result
    if first:
        return list(result)
    return [state[0], *result]


def both_cores(block):
    pairs = [[2 * i, 2 * i + 1] for i in range(CHIPS)]
    return lax.all_gather(block, "ctx", tiled=True, axis_index_groups=pairs)


def away(block, hops):
    route = []
    for chip in range(CHIPS):
        route.append((chip * 2, (chip + hops) % CHIPS * 2))
        route.append((chip * 2 + 1, (chip - hops) % CHIPS * 2 + 1))
    return lax.ppermute(block, "ctx", route)


def per_device(queries, keys, values, block_order):
    me = lax.axis_index("ctx")
    scalars = (block_order, me.astype(jnp.int32).reshape(1))
    chip = both_cores(jnp.concatenate([keys, values], axis=1))
    one = away(chip, 1)
    two = away(chip, 2)
    state = run_stage((0,), scalars, [queries, keys], chip)
    three = away(one, 2)
    state = run_stage((-1, 1), scalars, state, both_cores(one))
    half = lax.dynamic_slice_in_dim(two, me % 2 * ROWS, ROWS, 0)
    four = away(half, 2)
    state = run_stage((-2, 2), scalars, state, both_cores(two))
    state = run_stage((-3, 3), scalars, state, both_cores(three))
    return run_stage((4,), scalars, state, both_cores(four), last=True)


def solution(mesh):
    placed = P(("rep", "ctx"), "head")
    return jax.shard_map(
        per_device,
        mesh=mesh,
        in_specs=(placed, placed, placed, P("rep")),
        out_specs=placed,
        check_vma=False,
    )
```

```python
import functools
import math

import jax
import jax.numpy as jnp
from jax import lax
from jax.experimental import pallas as pl
from jax.experimental.pallas import tpu as pltpu
from jax.sharding import PartitionSpec as P

HEAD = 128
GROUP = 8
BLOCK = 160
ROWS = 2 * BLOCK
COLS = GROUP * BLOCK
CHIPS = 8
SUMROWS = HEAD + 16
SCALE = math.log2(math.e) / math.sqrt(HEAD)
NEG = -1e30
LIMIT = 2.0**100
CHIP, NEAR_2, NEAR_1, FAR_12, NEAR_3, FAR_3_AND_4 = range(6)
WIDEST = 4 * ROWS


def dot_nt(a, b):
    return lax.dot_general(a, b, (((1,), (1,)), ((), ())), preferred_element_type=jnp.float32)


def dot_nn(a, b):
    return lax.dot_general(a, b, (((1,), (0,)), ((), ())), preferred_element_type=jnp.float32)


def sources(part, me):
    chip, core = me // 2, lax.rem(me, 2)
    up = 1 - 2 * core

    def at(steps, which):
        return lax.rem(chip + steps + CHIPS, CHIPS) * 2 + which

    def both(steps):
        return [at(steps, 0), at(steps, 1)]

    if part == CHIP:
        return both(0)
    if part == NEAR_1:
        return both(-up)
    if part == NEAR_2:
        return both(-2 * up)
    if part == FAR_12:
        return both(up) + both(2 * up)
    if part == NEAR_3:
        return both(-3 * up)
    return both(3 * up) + [at(4, core), at(4, 1 - core)]


def block_positions(part, me, order_ref):
    positions = []
    for dev in sources(part, me):
        positions += [order_ref[dev * 2], order_ref[dev * 2 + 1]]
    return positions


def stage(part, *refs):
    first, last = part == CHIP, part == FAR_3_AND_4
    if first:
        me_ref, order_in, q_ref, kv_ref, qs_ref, seen_ref, m_out, acc_out, vt, order_ref, product, sems = refs
        stab = m_out
    elif last:
        qs_ref, seen_ref, stab, acc_in, kv_ref, o_ref, vt, seen_t, acc_out, m_out = refs
    else:
        qs_ref, seen_ref, stab, acc_in, kv_ref, m_out, acc_out, vt, seen_t = refs
    span = kv_ref.shape[0]

    if first:
        copies = [(order_in, order_ref)]
        for a in range(2):
            for h in range(GROUP):
                copies.append(
                    (
                        q_ref.at[pl.ds(a * BLOCK, BLOCK), pl.ds(h * HEAD, HEAD)],
                        qs_ref.at[pl.ds(a * COLS + h * BLOCK, BLOCK), :],
                    )
                )
        copies = [pltpu.make_async_copy(src, dst, sems.at[i]) for i, (src, dst) in enumerate(copies)]
        for copy in copies:
            copy.start()

    values_t = kv_ref[:, HEAD:].astype(jnp.float32).T

    if first:
        vt[:HEAD, :] = values_t.astype(jnp.bfloat16)
        vt[HEAD:, :] = jnp.ones((SUMROWS - HEAD, span), jnp.bfloat16)
        copies[0].wait()
        me = me_ref[0]
        lane = lax.broadcasted_iota(jnp.int32, (1, WIDEST), 1)
        seen_ref[...] = jnp.zeros(seen_ref.shape, jnp.float32)
        for other in range(NEAR_2, FAR_3_AND_4 + 1):
            lane_pos = jnp.zeros((1, WIDEST), jnp.int32)
            for j, pos in enumerate(block_positions(other, me, order_ref)):
                lane_pos = jnp.where(lane >= j * BLOCK, pos, lane_pos)
            for a in range(2):
                seen = jnp.where(lane_pos < order_ref[me * 2 + a], 1.0, 0.0)
                seen_ref[2 * other + a : 2 * other + a + 1, :] = seen
        row = lax.broadcasted_iota(jnp.int32, (span, 1), 0)
        key_pos = jnp.zeros((span, 1), jnp.int32)
        for j, pos in enumerate(block_positions(part, me, order_ref)):
            key_pos = jnp.where(row >= j * BLOCK, (pos - j) * BLOCK, key_pos)
        key_pos = key_pos + row
        for copy in copies[1:]:
            copy.wait()
        mine = lax.rem(me, 2) * ROWS
        for a in range(2):
            key_rows = kv_ref[pl.ds(pl.multiple_of(mine + a * BLOCK, BLOCK), BLOCK), :HEAD]
            for h in range(GROUP):
                rows = slice(a * COLS + h * BLOCK, a * COLS + (h + 1) * BLOCK)
                product[rows, :] = qs_ref[rows, :] * key_rows
        for c in range(0, 2 * COLS, 256):
            diag = dot_nt(jnp.ones((8, HEAD), jnp.bfloat16), product[c : c + 256, :])
            m_out[:, c : c + 256] = diag[:1] * SCALE

    def scores(a):
        return dot_nt(kv_ref[:, :HEAD], qs_ref[a * COLS : (a + 1) * COLS, :])

    over = jnp.zeros((1, 256), jnp.float32)
    ahead = scores(0)
    for a in range(2):
        cols = slice(a * COLS, (a + 1) * COLS)
        s, ahead = ahead, scores(1) if a == 0 else None
        p = jnp.exp2(s * SCALE - stab[:, cols])
        if first:
            token = lax.rem(lax.broadcasted_iota(jnp.int32, (1, COLS), 1), BLOCK) + order_ref[me * 2 + a] * BLOCK
            p = jnp.where(key_pos <= token, p, 0.0)
        else:
            seen = seen_ref[2 * part + a : 2 * part + a + 1, :span]
            vt[:HEAD, :] = (values_t * seen).astype(jnp.bfloat16)
            vt[HEAD:, :] = jnp.broadcast_to(seen, (SUMROWS - HEAD, span)).astype(jnp.bfloat16)
        new = dot_nn(vt[...], p.astype(jnp.bfloat16))
        if not first:
            new = new + acc_in[:, cols]
            m_out[:, cols] = stab[:, cols]
        acc_out[:, cols] = new
        mass = jnp.where(new[HEAD : HEAD + 1] <= LIMIT, 0.0, 1.0)
        for i in range(0, COLS, 256):
            over = over + mass[:, i : i + 256]

    @pl.when(jnp.sum(over) > 0.0)
    def _():
        if not first:
            seen_t[...] = seen_ref[...].T

        def tile(t, carry):
            a = t // (COLS // 256)
            cols = pl.ds(pl.multiple_of(t * 256, 256), 256)
            acc_out[:, cols] = jnp.zeros((SUMROWS, 256), jnp.float32) if first else acc_in[:, cols]
            m_out[:, cols] = stab[:, cols]

            def block(j, carry):
                rows = pl.ds(pl.multiple_of(j * BLOCK, BLOCK), BLOCK)
                s = dot_nt(kv_ref[rows, :HEAD], qs_ref[cols, :]) * SCALE
                if first:
                    col = (t - a * (COLS // 256)) * 256
                    token = lax.rem(lax.broadcasted_iota(jnp.int32, (1, 256), 1) + col, BLOCK)
                    key = lax.broadcasted_iota(jnp.int32, (BLOCK, 1), 0)
                    ahead = order_ref[me * 2 + a] - order_ref[me // 2 * 4 + j]
                    visible = key <= token + ahead * BLOCK
                else:
                    visible = jnp.where(a == 0, seen_t[rows, 2 * part : 2 * part + 1], seen_t[rows, 2 * part + 1 : 2 * part + 2])
                    visible = jnp.broadcast_to(visible, s.shape) > 0.5
                s = jnp.where(visible, s, NEG)
                m = m_out[:, cols]
                peak = jnp.maximum(m, jnp.max(s, axis=0, keepdims=True))
                p = jnp.exp2(s - peak).astype(jnp.bfloat16)
                value = jnp.concatenate(
                    [kv_ref[rows, HEAD:].astype(jnp.float32).T, jnp.ones((SUMROWS - HEAD, BLOCK), jnp.float32)], 0
                )
                acc_out[:, cols] = acc_out[:, cols] * jnp.exp2(m - peak) + dot_nn(value.astype(jnp.bfloat16), p)
                m_out[:, cols] = peak
                return carry

            return lax.fori_loop(0, span // BLOCK, block, carry)

        lax.fori_loop(0, 2 * COLS // 256, tile, 0)

    if last:
        for a in range(2):
            sums = acc_out[:, a * COLS : (a + 1) * COLS]
            full = (sums[:HEAD] * (1.0 / sums[HEAD : HEAD + 1])).T.astype(jnp.bfloat16)
            for h in range(GROUP):
                o_ref[a * BLOCK : (a + 1) * BLOCK, h * HEAD : (h + 1) * HEAD] = full[h * BLOCK : (h + 1) * BLOCK, :]


SUMS = jax.ShapeDtypeStruct((SUMROWS, 2 * COLS), jnp.float32)
TOPS = jax.ShapeDtypeStruct((1, 2 * COLS), jnp.float32)
LAID = jax.ShapeDtypeStruct((2 * COLS, HEAD), jnp.bfloat16)
SEEN = jax.ShapeDtypeStruct((16, WIDEST), jnp.float32)
VMEM = pl.BlockSpec(memory_space=pltpu.VMEM)
SMEM = pl.BlockSpec(memory_space=pltpu.SMEM)
ANY = pl.BlockSpec(memory_space=pl.ANY)


def run_stage(part, given, kv):
    span = kv.shape[0]
    scratch = [pltpu.VMEM((SUMROWS, span), jnp.bfloat16)]
    out, specs = (TOPS, SUMS), [VMEM] * 4
    if part == CHIP:
        out, specs = (LAID, SEEN, TOPS, SUMS), [SMEM, ANY, ANY]
        scratch += [pltpu.SMEM(given[1].shape, jnp.int32), pltpu.VMEM(LAID.shape, jnp.bfloat16)]
        scratch += [pltpu.SemaphoreType.DMA((1 + 2 * GROUP,))]
    else:
        scratch += [pltpu.VMEM(SEEN.shape[::-1], jnp.float32)]
    if part == FAR_3_AND_4:
        out = jax.ShapeDtypeStruct((ROWS, GROUP * HEAD), jnp.bfloat16)
        scratch += [pltpu.VMEM(SUMS.shape, jnp.float32), pltpu.VMEM(TOPS.shape, jnp.float32)]
    pairs = span * 2 * COLS
    result = pl.pallas_call(
        functools.partial(stage, part),
        out_shape=out,
        in_specs=specs + [VMEM],
        out_specs=jax.tree.map(lambda _: VMEM, out),
        scratch_shapes=scratch,
        compiler_params=pltpu.CompilerParams(vmem_limit_bytes=40 * 2**20),
        cost_estimate=pl.CostEstimate(
            flops=pairs * HEAD * 4, bytes_accessed=span * 512 + 4 * SUMS.size * 2, transcendentals=pairs
        ),
    )(*given, kv)
    if part in (CHIP, FAR_3_AND_4):
        return result
    return (*given[:2], *result)


def both_cores(block):
    pairs = [[2 * i, 2 * i + 1] for i in range(CHIPS)]
    return lax.all_gather(block, "ctx", tiled=True, axis_index_groups=pairs)


def other_core(block):
    return lax.ppermute(block, "ctx", [(i, i ^ 1) for i in range(2 * CHIPS)])


def away(block, hops):
    route = []
    for chip in range(CHIPS):
        route.append((chip * 2, (chip + hops) % CHIPS * 2))
        route.append((chip * 2 + 1, (chip - hops) % CHIPS * 2 + 1))
    return lax.ppermute(block, "ctx", route)


def after(block, state):
    block, _ = lax.optimization_barrier((block, state[-1]))
    return block


def per_device(queries, keys, values, block_order):
    me = lax.axis_index("ctx")
    chip = both_cores(jnp.concatenate([keys, values], axis=1))
    near_2 = away(chip, 2)
    near_1 = away(chip, 1)
    state = run_stage(CHIP, (me.astype(jnp.int32).reshape(1), block_order, queries), chip)
    near_2 = after(near_2, state)
    near_3 = away(near_2, 1)
    state = run_stage(NEAR_2, state, near_2)
    near_2 = after(near_2, state)
    near_1 = after(near_1, state)
    far_12 = other_core(jnp.concatenate([near_1, near_2], axis=0))
    state = run_stage(NEAR_1, state, near_1)
    half = lax.dynamic_slice_in_dim(after(near_2, state), me % 2 * ROWS, ROWS, 0)
    near_4 = away(half, 2)
    state = run_stage(FAR_12, state, far_12)
    near_3 = after(near_3, state)
    far_3 = other_core(near_3)
    state = run_stage(NEAR_3, state, near_3)
    near_4 = after(near_4, state)
    far_4 = other_core(near_4)
    return run_stage(FAR_3_AND_4, state, jnp.concatenate([far_3, near_4, far_4], axis=0))


def solution(mesh):
    placed = P(("rep", "ctx"), "head")
    return jax.shard_map(
        per_device,
        mesh=mesh,
        in_specs=(placed, placed, placed, P("rep")),
        out_specs=placed,
        check_vma=False,
    )
```

```python
import functools
import math

import jax
import jax.numpy as jnp
from jax import lax
from jax.experimental import pallas as pl
from jax.experimental.pallas import tpu as pltpu
from jax.sharding import PartitionSpec as P

HEAD = 128
GROUP = 8
BLOCK = 160
ROWS = 2 * BLOCK
COLS = GROUP * BLOCK
CHIPS = 8
SUMROWS = HEAD + 16
SCALE = math.log2(math.e) / math.sqrt(HEAD)
NEG = -1e30
LIMIT = 2.0**100
CHIP, NEAR_2, NEAR_1, FAR_12, NEAR_3, FAR_3_AND_4 = range(6)
WIDEST = 4 * ROWS


def dot_nt(a, b):
    return lax.dot_general(a, b, (((1,), (1,)), ((), ())), preferred_element_type=jnp.float32)


def dot_nn(a, b):
    return lax.dot_general(a, b, (((1,), (0,)), ((), ())), preferred_element_type=jnp.float32)


def sources(part, me):
    chip, core = me // 2, lax.rem(me, 2)
    up = 1 - 2 * core

    def at(steps, which):
        return lax.rem(chip + steps + CHIPS, CHIPS) * 2 + which

    def both(steps):
        return [at(steps, 0), at(steps, 1)]

    if part == CHIP:
        return both(0)
    if part == NEAR_1:
        return both(-up)
    if part == NEAR_2:
        return both(-2 * up)
    if part == FAR_12:
        return both(up) + both(2 * up)
    if part == NEAR_3:
        return both(-3 * up)
    return both(3 * up) + both(4)


def block_positions(part, me, order_ref):
    positions = []
    for dev in sources(part, me):
        positions += [order_ref[dev * 2], order_ref[dev * 2 + 1]]
    return positions


def stage(part, *refs):
    first, last = part == CHIP, part == FAR_3_AND_4
    if first:
        me_ref, order_in, q_ref, kv_ref, qs_ref, seen_ref, m_out, acc_out, vt, order_ref, product, sems = refs
        stab = m_out
    elif last:
        qs_ref, seen_ref, stab, acc_in, kv_ref, o_ref, vt, seen_t, acc_out, m_out = refs
    else:
        qs_ref, seen_ref, stab, acc_in, kv_ref, m_out, acc_out, vt, seen_t = refs
    span = kv_ref.shape[0]

    if first:
        copies = [(order_in, order_ref)]
        for a in range(2):
            for h in range(GROUP):
                copies.append(
                    (
                        q_ref.at[pl.ds(a * BLOCK, BLOCK), pl.ds(h * HEAD, HEAD)],
                        qs_ref.at[pl.ds(a * COLS + h * BLOCK, BLOCK), :],
                    )
                )
        copies = [pltpu.make_async_copy(src, dst, sems.at[i]) for i, (src, dst) in enumerate(copies)]
        for copy in copies:
            copy.start()

    values_t = kv_ref[:, HEAD:].astype(jnp.float32).T

    if first:
        vt[:HEAD, :] = values_t.astype(jnp.bfloat16)
        vt[HEAD:, :] = jnp.ones((SUMROWS - HEAD, span), jnp.bfloat16)
        copies[0].wait()
        me = me_ref[0]
        lane = lax.broadcasted_iota(jnp.int32, (1, WIDEST), 1)
        seen_ref[...] = jnp.zeros(seen_ref.shape, jnp.float32)
        for other in range(NEAR_2, FAR_3_AND_4 + 1):
            lane_pos = jnp.zeros((1, WIDEST), jnp.int32)
            for j, pos in enumerate(block_positions(other, me, order_ref)):
                lane_pos = jnp.where(lane >= j * BLOCK, pos, lane_pos)
            for a in range(2):
                seen = jnp.where(lane_pos < order_ref[me * 2 + a], 1.0, 0.0)
                seen_ref[2 * other + a : 2 * other + a + 1, :] = seen
        row = lax.broadcasted_iota(jnp.int32, (span, 1), 0)
        key_pos = jnp.zeros((span, 1), jnp.int32)
        for j, pos in enumerate(block_positions(part, me, order_ref)):
            key_pos = jnp.where(row >= j * BLOCK, (pos - j) * BLOCK, key_pos)
        key_pos = key_pos + row
        for copy in copies[1:]:
            copy.wait()
        mine = lax.rem(me, 2) * ROWS
        for a in range(2):
            key_rows = kv_ref[pl.ds(pl.multiple_of(mine + a * BLOCK, BLOCK), BLOCK), :HEAD]
            for h in range(GROUP):
                rows = slice(a * COLS + h * BLOCK, a * COLS + (h + 1) * BLOCK)
                product[rows, :] = qs_ref[rows, :] * key_rows
        for c in range(0, 2 * COLS, 256):
            diag = dot_nt(jnp.ones((8, HEAD), jnp.bfloat16), product[c : c + 256, :])
            m_out[:, c : c + 256] = diag[:1] * SCALE

    def scores(a):
        return dot_nt(kv_ref[:, :HEAD], qs_ref[a * COLS : (a + 1) * COLS, :])

    over = jnp.zeros((1, 256), jnp.float32)
    ahead = scores(0)
    for a in range(2):
        cols = slice(a * COLS, (a + 1) * COLS)
        s, ahead = ahead, scores(1) if a == 0 else None
        p = jnp.exp2(s * SCALE - stab[:, cols])
        if first:
            token = lax.rem(lax.broadcasted_iota(jnp.int32, (1, COLS), 1), BLOCK) + order_ref[me * 2 + a] * BLOCK
            p = jnp.where(key_pos <= token, p, 0.0)
        else:
            seen = seen_ref[2 * part + a : 2 * part + a + 1, :span]
            vt[:HEAD, :] = (values_t * seen).astype(jnp.bfloat16)
            vt[HEAD:, :] = jnp.broadcast_to(seen, (SUMROWS - HEAD, span)).astype(jnp.bfloat16)
        new = dot_nn(vt[...], p.astype(jnp.bfloat16))
        if not first:
            new = new + acc_in[:, cols]
            m_out[:, cols] = stab[:, cols]
        acc_out[:, cols] = new
        mass = jnp.where(new[HEAD : HEAD + 1] <= LIMIT, 0.0, 1.0)
        for i in range(0, COLS, 256):
            over = over + mass[:, i : i + 256]

    @pl.when(jnp.sum(over) > 0.0)
    def _():
        if not first:
            seen_t[...] = seen_ref[...].T

        def tile(t, carry):
            a = t // (COLS // 256)
            cols = pl.ds(pl.multiple_of(t * 256, 256), 256)
            acc_out[:, cols] = jnp.zeros((SUMROWS, 256), jnp.float32) if first else acc_in[:, cols]
            m_out[:, cols] = stab[:, cols]

            def block(j, carry):
                rows = pl.ds(pl.multiple_of(j * BLOCK, BLOCK), BLOCK)
                s = dot_nt(kv_ref[rows, :HEAD], qs_ref[cols, :]) * SCALE
                if first:
                    col = (t - a * (COLS // 256)) * 256
                    token = lax.rem(lax.broadcasted_iota(jnp.int32, (1, 256), 1) + col, BLOCK)
                    key = lax.broadcasted_iota(jnp.int32, (BLOCK, 1), 0)
                    ahead = order_ref[me * 2 + a] - order_ref[me // 2 * 4 + j]
                    visible = key <= token + ahead * BLOCK
                else:
                    visible = jnp.where(a == 0, seen_t[rows, 2 * part : 2 * part + 1], seen_t[rows, 2 * part + 1 : 2 * part + 2])
                    visible = jnp.broadcast_to(visible, s.shape) > 0.5
                s = jnp.where(visible, s, NEG)
                m = m_out[:, cols]
                peak = jnp.maximum(m, jnp.max(s, axis=0, keepdims=True))
                p = jnp.exp2(s - peak).astype(jnp.bfloat16)
                value = jnp.concatenate(
                    [kv_ref[rows, HEAD:].astype(jnp.float32).T, jnp.ones((SUMROWS - HEAD, BLOCK), jnp.float32)], 0
                )
                acc_out[:, cols] = acc_out[:, cols] * jnp.exp2(m - peak) + dot_nn(value.astype(jnp.bfloat16), p)
                m_out[:, cols] = peak
                return carry

            return lax.fori_loop(0, span // BLOCK, block, carry)

        lax.fori_loop(0, 2 * COLS // 256, tile, 0)

    if last:
        for a in range(2):
            sums = acc_out[:, a * COLS : (a + 1) * COLS]
            full = (sums[:HEAD] * (1.0 / sums[HEAD : HEAD + 1])).T.astype(jnp.bfloat16)
            for h in range(GROUP):
                o_ref[a * BLOCK : (a + 1) * BLOCK, h * HEAD : (h + 1) * HEAD] = full[h * BLOCK : (h + 1) * BLOCK, :]


SUMS = jax.ShapeDtypeStruct((SUMROWS, 2 * COLS), jnp.float32)
TOPS = jax.ShapeDtypeStruct((1, 2 * COLS), jnp.float32)
LAID = jax.ShapeDtypeStruct((2 * COLS, HEAD), jnp.bfloat16)
SEEN = jax.ShapeDtypeStruct((16, WIDEST), jnp.float32)
VMEM = pl.BlockSpec(memory_space=pltpu.VMEM)
SMEM = pl.BlockSpec(memory_space=pltpu.SMEM)
ANY = pl.BlockSpec(memory_space=pl.ANY)


def run_stage(part, given, kv):
    span = kv.shape[0]
    scratch = [pltpu.VMEM((SUMROWS, span), jnp.bfloat16)]
    out, specs = (TOPS, SUMS), [VMEM] * 4
    if part == CHIP:
        out, specs = (LAID, SEEN, TOPS, SUMS), [SMEM, ANY, ANY]
        scratch += [pltpu.SMEM(given[1].shape, jnp.int32), pltpu.VMEM(LAID.shape, jnp.bfloat16)]
        scratch += [pltpu.SemaphoreType.DMA((1 + 2 * GROUP,))]
    else:
        scratch += [pltpu.VMEM(SEEN.shape[::-1], jnp.float32)]
    if part == FAR_3_AND_4:
        out = jax.ShapeDtypeStruct((ROWS, GROUP * HEAD), jnp.bfloat16)
        scratch += [pltpu.VMEM(SUMS.shape, jnp.float32), pltpu.VMEM(TOPS.shape, jnp.float32)]
    pairs = span * 2 * COLS
    result = pl.pallas_call(
        functools.partial(stage, part),
        out_shape=out,
        in_specs=specs + [VMEM],
        out_specs=jax.tree.map(lambda _: VMEM, out),
        scratch_shapes=scratch,
        compiler_params=pltpu.CompilerParams(vmem_limit_bytes=32 * 2**20),
        cost_estimate=pl.CostEstimate(
            flops=pairs * HEAD * 4, bytes_accessed=span * 512 + 4 * SUMS.size * 2, transcendentals=pairs
        ),
    )(*given, kv)
    if part in (CHIP, FAR_3_AND_4):
        return result
    return (*given[:2], *result)


def both_cores(block):
    pairs = [[2 * i, 2 * i + 1] for i in range(CHIPS)]
    return lax.all_gather(block, "ctx", tiled=True, axis_index_groups=pairs)


def other_core(block):
    return lax.ppermute(block, "ctx", [(i, i ^ 1) for i in range(2 * CHIPS)])


def away(block, hops):
    route = []
    for chip in range(CHIPS):
        route.append((chip * 2, (chip + hops) % CHIPS * 2))
        route.append((chip * 2 + 1, (chip - hops) % CHIPS * 2 + 1))
    return lax.ppermute(block, "ctx", route)


def after(block, state):
    block, _ = lax.optimization_barrier((block, state[-1]))
    return block


def per_device(queries, keys, values, block_order):
    me = lax.axis_index("ctx")
    chip = both_cores(jnp.concatenate([keys, values], axis=1))
    near_2 = away(chip, 2)
    near_1 = away(chip, 1)
    state = run_stage(CHIP, (me.astype(jnp.int32).reshape(1), block_order, queries), chip)
    near_2 = after(near_2, state)
    near_3 = away(near_2, 1)
    state = run_stage(NEAR_2, state, near_2)
    near_2 = after(near_2, state)
    near_1 = after(near_1, state)
    far_12 = other_core(jnp.concatenate([near_1, near_2], axis=0))
    state = run_stage(NEAR_1, state, near_1)
    half = lax.dynamic_slice_in_dim(after(near_2, state), me % 2 * ROWS, ROWS, 0)
    near_4 = away(half, 2)
    state = run_stage(FAR_12, state, far_12)
    near_3 = after(near_3, state)
    far_3 = other_core(near_3)
    state = run_stage(NEAR_3, state, near_3)
    near_4 = after(near_4, state)
    return run_stage(FAR_3_AND_4, state, jnp.concatenate([far_3, both_cores(near_4)], axis=0))


def solution(mesh):
    placed = P(("rep", "ctx"), "head")
    return jax.shard_map(
        per_device,
        mesh=mesh,
        in_specs=(placed, placed, placed, P("rep")),
        out_specs=placed,
        check_vma=False,
    )
```

```python
import functools
import math

import jax
import jax.numpy as jnp
from jax import lax
from jax.experimental import pallas as pl
from jax.experimental.pallas import tpu as pltpu
from jax.sharding import PartitionSpec as P

HEAD = 128
GROUP = 8
BLOCK = 160
ROWS = 2 * BLOCK
COLS = GROUP * BLOCK
CHIPS = 8
SUMROWS = HEAD + 16
SCALE = math.log2(math.e) / math.sqrt(HEAD)
NEG = -1e30
LIMIT = 2.0**100
CHIP, NEAR_2, NEAR_1, FAR_12, NEAR_3, FAR_3_NEAR_4, FAR_4 = range(7)
WIDEST = 4 * ROWS


def dot_nt(a, b):
    return lax.dot_general(a, b, (((1,), (1,)), ((), ())), preferred_element_type=jnp.float32)


def dot_nn(a, b):
    return lax.dot_general(a, b, (((1,), (0,)), ((), ())), preferred_element_type=jnp.float32)


def sources(part, me):
    chip, core = me // 2, lax.rem(me, 2)
    up = 1 - 2 * core

    def at(steps, which):
        return lax.rem(chip + steps + CHIPS, CHIPS) * 2 + which

    def both(steps):
        return [at(steps, 0), at(steps, 1)]

    if part == CHIP:
        return both(0)
    if part == NEAR_1:
        return both(-up)
    if part == NEAR_2:
        return both(-2 * up)
    if part == FAR_12:
        return both(up) + both(2 * up)
    if part == NEAR_3:
        return both(-3 * up)
    if part == FAR_3_NEAR_4:
        return both(3 * up) + [at(4, core)]
    return [at(4, 1 - core)]


def block_positions(part, me, order_ref):
    positions = []
    for dev in sources(part, me):
        positions += [order_ref[dev * 2], order_ref[dev * 2 + 1]]
    return positions


def stage(part, *refs):
    first, last = part == CHIP, part == FAR_4
    if first:
        me_ref, order_in, q_ref, kv_ref, qs_ref, seen_ref, m_out, acc_out, vt, order_ref, product, sems = refs
        stab = m_out
    elif last:
        qs_ref, seen_ref, stab, acc_in, kv_ref, o_ref, vt, seen_t, acc_out, m_out = refs
    else:
        qs_ref, seen_ref, stab, acc_in, kv_ref, m_out, acc_out, vt, seen_t = refs
    span = kv_ref.shape[0]

    if first:
        copies = [(order_in, order_ref)]
        for a in range(2):
            for h in range(GROUP):
                copies.append(
                    (
                        q_ref.at[pl.ds(a * BLOCK, BLOCK), pl.ds(h * HEAD, HEAD)],
                        qs_ref.at[pl.ds(a * COLS + h * BLOCK, BLOCK), :],
                    )
                )
        copies = [pltpu.make_async_copy(src, dst, sems.at[i]) for i, (src, dst) in enumerate(copies)]
        for copy in copies:
            copy.start()

    values_t = kv_ref[:, HEAD:].astype(jnp.float32).T

    if first:
        vt[:HEAD, :] = values_t.astype(jnp.bfloat16)
        vt[HEAD:, :] = jnp.ones((SUMROWS - HEAD, span), jnp.bfloat16)
        copies[0].wait()
        me = me_ref[0]
        lane = lax.broadcasted_iota(jnp.int32, (1, WIDEST), 1)
        seen_ref[...] = jnp.zeros(seen_ref.shape, jnp.float32)
        for other in range(NEAR_2, FAR_4 + 1):
            lane_pos = jnp.zeros((1, WIDEST), jnp.int32)
            for j, pos in enumerate(block_positions(other, me, order_ref)):
                lane_pos = jnp.where(lane >= j * BLOCK, pos, lane_pos)
            for a in range(2):
                seen = jnp.where(lane_pos < order_ref[me * 2 + a], 1.0, 0.0)
                seen_ref[2 * other + a : 2 * other + a + 1, :] = seen
        row = lax.broadcasted_iota(jnp.int32, (span, 1), 0)
        key_pos = jnp.zeros((span, 1), jnp.int32)
        for j, pos in enumerate(block_positions(part, me, order_ref)):
            key_pos = jnp.where(row >= j * BLOCK, (pos - j) * BLOCK, key_pos)
        key_pos = key_pos + row
        for copy in copies[1:]:
            copy.wait()
        mine = lax.rem(me, 2) * ROWS
        for a in range(2):
            key_rows = kv_ref[pl.ds(pl.multiple_of(mine + a * BLOCK, BLOCK), BLOCK), :HEAD]
            for h in range(GROUP):
                rows = slice(a * COLS + h * BLOCK, a * COLS + (h + 1) * BLOCK)
                product[rows, :] = qs_ref[rows, :] * key_rows
        for c in range(0, 2 * COLS, 256):
            diag = dot_nt(jnp.ones((8, HEAD), jnp.bfloat16), product[c : c + 256, :])
            m_out[:, c : c + 256] = diag[:1] * SCALE

    def scores(a):
        return dot_nt(kv_ref[:, :HEAD], qs_ref[a * COLS : (a + 1) * COLS, :])

    over = jnp.zeros((1, 256), jnp.float32)
    ahead = scores(0)
    for a in range(2):
        cols = slice(a * COLS, (a + 1) * COLS)
        s, ahead = ahead, scores(1) if a == 0 else None
        p = jnp.exp2(s * SCALE - stab[:, cols])
        if first:
            token = lax.rem(lax.broadcasted_iota(jnp.int32, (1, COLS), 1), BLOCK) + order_ref[me * 2 + a] * BLOCK
            p = jnp.where(key_pos <= token, p, 0.0)
        else:
            seen = seen_ref[2 * part + a : 2 * part + a + 1, :span]
            vt[:HEAD, :] = (values_t * seen).astype(jnp.bfloat16)
            vt[HEAD:, :] = jnp.broadcast_to(seen, (SUMROWS - HEAD, span)).astype(jnp.bfloat16)
        new = dot_nn(vt[...], p.astype(jnp.bfloat16))
        if not first:
            new = new + acc_in[:, cols]
            m_out[:, cols] = stab[:, cols]
        acc_out[:, cols] = new
        mass = jnp.where(new[HEAD : HEAD + 1] <= LIMIT, 0.0, 1.0)
        for i in range(0, COLS, 256):
            over = over + mass[:, i : i + 256]

    @pl.when(jnp.sum(over) > 0.0)
    def _():
        if not first:
            seen_t[...] = seen_ref[...].T

        def tile(t, carry):
            a = t // (COLS // 256)
            cols = pl.ds(pl.multiple_of(t * 256, 256), 256)
            acc_out[:, cols] = jnp.zeros((SUMROWS, 256), jnp.float32) if first else acc_in[:, cols]
            m_out[:, cols] = stab[:, cols]

            def block(j, carry):
                rows = pl.ds(pl.multiple_of(j * BLOCK, BLOCK), BLOCK)
                s = dot_nt(kv_ref[rows, :HEAD], qs_ref[cols, :]) * SCALE
                if first:
                    col = (t - a * (COLS // 256)) * 256
                    token = lax.rem(lax.broadcasted_iota(jnp.int32, (1, 256), 1) + col, BLOCK)
                    key = lax.broadcasted_iota(jnp.int32, (BLOCK, 1), 0)
                    ahead = order_ref[me * 2 + a] - order_ref[me // 2 * 4 + j]
                    visible = key <= token + ahead * BLOCK
                else:
                    visible = jnp.where(a == 0, seen_t[rows, 2 * part : 2 * part + 1], seen_t[rows, 2 * part + 1 : 2 * part + 2])
                    visible = jnp.broadcast_to(visible, s.shape) > 0.5
                s = jnp.where(visible, s, NEG)
                m = m_out[:, cols]
                peak = jnp.maximum(m, jnp.max(s, axis=0, keepdims=True))
                p = jnp.exp2(s - peak).astype(jnp.bfloat16)
                value = jnp.concatenate(
                    [kv_ref[rows, HEAD:].astype(jnp.float32).T, jnp.ones((SUMROWS - HEAD, BLOCK), jnp.float32)], 0
                )
                acc_out[:, cols] = acc_out[:, cols] * jnp.exp2(m - peak) + dot_nn(value.astype(jnp.bfloat16), p)
                m_out[:, cols] = peak
                return carry

            return lax.fori_loop(0, span // BLOCK, block, carry)

        lax.fori_loop(0, 2 * COLS // 256, tile, 0)

    if last:
        for a in range(2):
            sums = acc_out[:, a * COLS : (a + 1) * COLS]
            full = (sums[:HEAD] * (1.0 / sums[HEAD : HEAD + 1])).T.astype(jnp.bfloat16)
            for h in range(GROUP):
                o_ref[a * BLOCK : (a + 1) * BLOCK, h * HEAD : (h + 1) * HEAD] = full[h * BLOCK : (h + 1) * BLOCK, :]


SUMS = jax.ShapeDtypeStruct((SUMROWS, 2 * COLS), jnp.float32)
TOPS = jax.ShapeDtypeStruct((1, 2 * COLS), jnp.float32)
LAID = jax.ShapeDtypeStruct((2 * COLS, HEAD), jnp.bfloat16)
SEEN = jax.ShapeDtypeStruct((16, WIDEST), jnp.float32)
VMEM = pl.BlockSpec(memory_space=pltpu.VMEM)
SMEM = pl.BlockSpec(memory_space=pltpu.SMEM)
ANY = pl.BlockSpec(memory_space=pl.ANY)


def run_stage(part, given, kv):
    span = kv.shape[0]
    scratch = [pltpu.VMEM((SUMROWS, span), jnp.bfloat16)]
    out, specs = (TOPS, SUMS), [VMEM] * 4
    if part == CHIP:
        out, specs = (LAID, SEEN, TOPS, SUMS), [SMEM, ANY, ANY]
        scratch += [pltpu.SMEM(given[1].shape, jnp.int32), pltpu.VMEM(LAID.shape, jnp.bfloat16)]
        scratch += [pltpu.SemaphoreType.DMA((1 + 2 * GROUP,))]
    else:
        scratch += [pltpu.VMEM(SEEN.shape[::-1], jnp.float32)]
    if part == FAR_4:
        out = jax.ShapeDtypeStruct((ROWS, GROUP * HEAD), jnp.bfloat16)
        scratch += [pltpu.VMEM(SUMS.shape, jnp.float32), pltpu.VMEM(TOPS.shape, jnp.float32)]
    pairs = 1 if part == NEAR_3 else span * 2 * COLS
    result = pl.pallas_call(
        functools.partial(stage, part),
        out_shape=out,
        in_specs=specs + [VMEM],
        out_specs=jax.tree.map(lambda _: VMEM, out),
        scratch_shapes=scratch,
        compiler_params=pltpu.CompilerParams(vmem_limit_bytes=40 * 2**20),
        cost_estimate=pl.CostEstimate(flops=pairs * HEAD * 4, bytes_accessed=pairs, transcendentals=pairs),
    )(*given, kv)
    if part in (CHIP, FAR_4):
        return result
    return (*given[:2], *result)


def both_cores(block):
    pairs = [[2 * i, 2 * i + 1] for i in range(CHIPS)]
    return lax.all_gather(block, "ctx", tiled=True, axis_index_groups=pairs)


def other_core(block):
    return lax.ppermute(block, "ctx", [(i, i ^ 1) for i in range(2 * CHIPS)])


def away(block, hops):
    route = []
    for chip in range(CHIPS):
        route.append((chip * 2, (chip + hops) % CHIPS * 2))
        route.append((chip * 2 + 1, (chip - hops) % CHIPS * 2 + 1))
    return lax.ppermute(block, "ctx", route)


def after(block, state):
    block, _ = lax.optimization_barrier((block, state[-1]))
    return block


def per_device(queries, keys, values, block_order):
    me = lax.axis_index("ctx")
    chip = both_cores(jnp.concatenate([keys, values], axis=1))
    near_2 = away(chip, 2)
    near_1 = away(chip, 1)
    state = run_stage(CHIP, (me.astype(jnp.int32).reshape(1), block_order, queries), chip)
    near_2 = after(near_2, state)
    near_3 = away(near_2, 1)
    state = run_stage(NEAR_2, state, near_2)
    near_2 = after(near_2, state)
    near_1 = after(near_1, state)
    far_12 = other_core(jnp.concatenate([near_1, near_2], axis=0))
    state = run_stage(NEAR_1, state, near_1)
    half = lax.dynamic_slice_in_dim(after(near_2, state), me % 2 * ROWS, ROWS, 0)
    near_4 = away(half, 2)
    state = run_stage(FAR_12, state, far_12)
    near_3 = after(near_3, state)
    far_3 = other_core(near_3)
    state = run_stage(NEAR_3, state, near_3)
    near_4 = after(near_4, state)
    far_4 = other_core(near_4)
    state = run_stage(FAR_3_NEAR_4, state, jnp.concatenate([far_3, near_4], axis=0))
    return run_stage(FAR_4, state, far_4)


def solution(mesh):
    placed = P(("rep", "ctx"), "head")
    return jax.shard_map(
        per_device,
        mesh=mesh,
        in_specs=(placed, placed, placed, P("rep")),
        out_specs=placed,
        check_vma=False,
    )
```

```python
import functools
import math

import jax
import jax.numpy as jnp
from jax import lax
from jax.experimental import pallas as pl
from jax.experimental.pallas import tpu as pltpu
from jax.sharding import PartitionSpec as P

HEAD = 128
GROUP = 8
BLOCK = 160
ROWS = 2 * BLOCK
COLS = GROUP * BLOCK
CHIPS = 8
SUMROWS = HEAD + 16
SCALE = math.log2(math.e) / math.sqrt(HEAD)
NEG = -1e30
LIMIT = 2.0**100
CHIP, NEAR_2, NEAR_1, FAR_12, NEAR_3, FAR_3_NEAR_4, FAR_4 = range(7)
WIDEST = 4 * ROWS


def dot_nt(a, b):
    return lax.dot_general(a, b, (((1,), (1,)), ((), ())), preferred_element_type=jnp.float32)


def dot_nn(a, b):
    return lax.dot_general(a, b, (((1,), (0,)), ((), ())), preferred_element_type=jnp.float32)


def sources(part, me):
    chip, core = me // 2, lax.rem(me, 2)
    up = 1 - 2 * core

    def at(steps, which):
        return lax.rem(chip + steps + CHIPS, CHIPS) * 2 + which

    def both(steps):
        return [at(steps, 0), at(steps, 1)]

    if part == CHIP:
        return both(0)
    if part == NEAR_1:
        return both(-up)
    if part == NEAR_2:
        return both(-2 * up)
    if part == FAR_12:
        return both(up) + both(2 * up)
    if part == NEAR_3:
        return both(-3 * up)
    if part == FAR_3_NEAR_4:
        return both(3 * up) + [at(4, core)]
    return [at(4, 1 - core)]


def block_positions(part, me, order_ref):
    positions = []
    for dev in sources(part, me):
        positions += [order_ref[dev * 2], order_ref[dev * 2 + 1]]
    return positions


def stage(part, *refs):
    first, last = part == CHIP, part == FAR_4
    if first:
        me_ref, order_in, q_ref, kv_ref, qs_ref, seen_ref, m_out, acc_out, vt, order_ref, product, sems = refs
        stab = m_out
    elif last:
        qs_ref, seen_ref, stab, acc_in, kv_ref, o_ref, vt, seen_t, acc_out, m_out = refs
    else:
        qs_ref, seen_ref, stab, acc_in, kv_ref, m_out, acc_out, vt, seen_t = refs
    span = kv_ref.shape[0]

    if first:
        copies = [(order_in, order_ref)]
        for a in range(2):
            for h in range(GROUP):
                copies.append(
                    (
                        q_ref.at[pl.ds(a * BLOCK, BLOCK), pl.ds(h * HEAD, HEAD)],
                        qs_ref.at[pl.ds(a * COLS + h * BLOCK, BLOCK), :],
                    )
                )
        copies = [pltpu.make_async_copy(src, dst, sems.at[i]) for i, (src, dst) in enumerate(copies)]
        for copy in copies:
            copy.start()

    values_t = kv_ref[:, HEAD:].astype(jnp.float32).T

    if first:
        vt[:HEAD, :] = values_t.astype(jnp.bfloat16)
        vt[HEAD:, :] = jnp.ones((SUMROWS - HEAD, span), jnp.bfloat16)
        copies[0].wait()
        me = me_ref[0]
        lane = lax.broadcasted_iota(jnp.int32, (1, WIDEST), 1)
        seen_ref[...] = jnp.zeros(seen_ref.shape, jnp.float32)
        for other in range(NEAR_2, FAR_4 + 1):
            lane_pos = jnp.zeros((1, WIDEST), jnp.int32)
            for j, pos in enumerate(block_positions(other, me, order_ref)):
                lane_pos = jnp.where(lane >= j * BLOCK, pos, lane_pos)
            for a in range(2):
                seen = jnp.where(lane_pos < order_ref[me * 2 + a], 1.0, 0.0)
                seen_ref[2 * other + a : 2 * other + a + 1, :] = seen
        row = lax.broadcasted_iota(jnp.int32, (span, 1), 0)
        key_pos = jnp.zeros((span, 1), jnp.int32)
        for j, pos in enumerate(block_positions(part, me, order_ref)):
            key_pos = jnp.where(row >= j * BLOCK, (pos - j) * BLOCK, key_pos)
        key_pos = key_pos + row
        for copy in copies[1:]:
            copy.wait()
        mine = lax.rem(me, 2) * ROWS
        for a in range(2):
            key_rows = kv_ref[pl.ds(pl.multiple_of(mine + a * BLOCK, BLOCK), BLOCK), :HEAD]
            for h in range(GROUP):
                rows = slice(a * COLS + h * BLOCK, a * COLS + (h + 1) * BLOCK)
                product[rows, :] = qs_ref[rows, :] * key_rows
        for c in range(0, 2 * COLS, 256):
            diag = dot_nt(jnp.ones((8, HEAD), jnp.bfloat16), product[c : c + 256, :])
            m_out[:, c : c + 256] = diag[:1] * SCALE

    def scores(a):
        return dot_nt(kv_ref[:, :HEAD], qs_ref[a * COLS : (a + 1) * COLS, :])

    over = jnp.zeros((1, 256), jnp.float32)
    ahead = scores(0)
    for a in range(2):
        cols = slice(a * COLS, (a + 1) * COLS)
        s, ahead = ahead, scores(1) if a == 0 else None
        p = jnp.exp2(s * SCALE - stab[:, cols])
        if first:
            token = lax.rem(lax.broadcasted_iota(jnp.int32, (1, COLS), 1), BLOCK) + order_ref[me * 2 + a] * BLOCK
            p = jnp.where(key_pos <= token, p, 0.0)
        else:
            seen = seen_ref[2 * part + a : 2 * part + a + 1, :span]
            vt[:HEAD, :] = (values_t * seen).astype(jnp.bfloat16)
            vt[HEAD:, :] = jnp.broadcast_to(seen, (SUMROWS - HEAD, span)).astype(jnp.bfloat16)
        new = dot_nn(vt[...], p.astype(jnp.bfloat16))
        if not first:
            new = new + acc_in[:, cols]
            m_out[:, cols] = stab[:, cols]
        acc_out[:, cols] = new
        mass = jnp.where(new[HEAD : HEAD + 1] <= LIMIT, 0.0, 1.0)
        for i in range(0, COLS, 256):
            over = over + mass[:, i : i + 256]

    @pl.when(jnp.sum(over) > 0.0)
    def _():
        if not first:
            seen_t[...] = seen_ref[...].T

        def tile(t, carry):
            a = t // (COLS // 256)
            cols = pl.ds(pl.multiple_of(t * 256, 256), 256)
            acc_out[:, cols] = jnp.zeros((SUMROWS, 256), jnp.float32) if first else acc_in[:, cols]
            m_out[:, cols] = stab[:, cols]

            def block(j, carry):
                rows = pl.ds(pl.multiple_of(j * BLOCK, BLOCK), BLOCK)
                s = dot_nt(kv_ref[rows, :HEAD], qs_ref[cols, :]) * SCALE
                if first:
                    col = (t - a * (COLS // 256)) * 256
                    token = lax.rem(lax.broadcasted_iota(jnp.int32, (1, 256), 1) + col, BLOCK)
                    key = lax.broadcasted_iota(jnp.int32, (BLOCK, 1), 0)
                    ahead = order_ref[me * 2 + a] - order_ref[me // 2 * 4 + j]
                    visible = key <= token + ahead * BLOCK
                else:
                    visible = jnp.where(a == 0, seen_t[rows, 2 * part : 2 * part + 1], seen_t[rows, 2 * part + 1 : 2 * part + 2])
                    visible = jnp.broadcast_to(visible, s.shape) > 0.5
                s = jnp.where(visible, s, NEG)
                m = m_out[:, cols]
                peak = jnp.maximum(m, jnp.max(s, axis=0, keepdims=True))
                p = jnp.exp2(s - peak).astype(jnp.bfloat16)
                value = jnp.concatenate(
                    [kv_ref[rows, HEAD:].astype(jnp.float32).T, jnp.ones((SUMROWS - HEAD, BLOCK), jnp.float32)], 0
                )
                acc_out[:, cols] = acc_out[:, cols] * jnp.exp2(m - peak) + dot_nn(value.astype(jnp.bfloat16), p)
                m_out[:, cols] = peak
                return carry

            return lax.fori_loop(0, span // BLOCK, block, carry)

        lax.fori_loop(0, 2 * COLS // 256, tile, 0)

    if last:
        for a in range(2):
            sums = acc_out[:, a * COLS : (a + 1) * COLS]
            full = (sums[:HEAD] * (1.0 / sums[HEAD : HEAD + 1])).T.astype(jnp.bfloat16)
            for h in range(GROUP):
                o_ref[a * BLOCK : (a + 1) * BLOCK, h * HEAD : (h + 1) * HEAD] = full[h * BLOCK : (h + 1) * BLOCK, :]


SUMS = jax.ShapeDtypeStruct((SUMROWS, 2 * COLS), jnp.float32)
TOPS = jax.ShapeDtypeStruct((1, 2 * COLS), jnp.float32)
LAID = jax.ShapeDtypeStruct((2 * COLS, HEAD), jnp.bfloat16)
SEEN = jax.ShapeDtypeStruct((16, WIDEST), jnp.float32)
VMEM = pl.BlockSpec(memory_space=pltpu.VMEM)
SMEM = pl.BlockSpec(memory_space=pltpu.SMEM)
ANY = pl.BlockSpec(memory_space=pl.ANY)


def run_stage(part, given, kv):
    span = kv.shape[0]
    scratch = [pltpu.VMEM((SUMROWS, span), jnp.bfloat16)]
    out, specs = (TOPS, SUMS), [VMEM] * 4
    if part == CHIP:
        out, specs = (LAID, SEEN, TOPS, SUMS), [SMEM, ANY, ANY]
        scratch += [pltpu.SMEM(given[1].shape, jnp.int32), pltpu.VMEM(LAID.shape, jnp.bfloat16)]
        scratch += [pltpu.SemaphoreType.DMA((1 + 2 * GROUP,))]
    else:
        scratch += [pltpu.VMEM(SEEN.shape[::-1], jnp.float32)]
    if part == FAR_4:
        out = jax.ShapeDtypeStruct((ROWS, GROUP * HEAD), jnp.bfloat16)
        scratch += [pltpu.VMEM(SUMS.shape, jnp.float32), pltpu.VMEM(TOPS.shape, jnp.float32)]
    result = pl.pallas_call(
        functools.partial(stage, part),
        out_shape=out,
        in_specs=specs + [VMEM],
        out_specs=jax.tree.map(lambda _: VMEM, out),
        scratch_shapes=scratch,
        compiler_params=pltpu.CompilerParams(vmem_limit_bytes=40 * 2**20),
        cost_estimate=pl.CostEstimate(flops=1, bytes_accessed=1, transcendentals=0),
    )(*given, kv)
    if part in (CHIP, FAR_4):
        return result
    return (*given[:2], *result)


def both_cores(block):
    pairs = [[2 * i, 2 * i + 1] for i in range(CHIPS)]
    return lax.all_gather(block, "ctx", tiled=True, axis_index_groups=pairs)


def other_core(block):
    return lax.ppermute(block, "ctx", [(i, i ^ 1) for i in range(2 * CHIPS)])


def away(block, hops):
    route = []
    for chip in range(CHIPS):
        route.append((chip * 2, (chip + hops) % CHIPS * 2))
        route.append((chip * 2 + 1, (chip - hops) % CHIPS * 2 + 1))
    return lax.ppermute(block, "ctx", route)


def after(block, state):
    block, _ = lax.optimization_barrier((block, state[-1]))
    return block


def per_device(queries, keys, values, block_order):
    me = lax.axis_index("ctx")
    chip = both_cores(jnp.concatenate([keys, values], axis=1))
    near_2 = away(chip, 2)
    near_1 = away(chip, 1)
    state = run_stage(CHIP, (me.astype(jnp.int32).reshape(1), block_order, queries), chip)
    near_2 = after(near_2, state)
    near_3 = away(near_2, 1)
    state = run_stage(NEAR_2, state, near_2)
    near_2 = after(near_2, state)
    near_1 = after(near_1, state)
    far_12 = other_core(jnp.concatenate([near_1, near_2], axis=0))
    state = run_stage(NEAR_1, state, near_1)
    half = lax.dynamic_slice_in_dim(after(near_2, state), me % 2 * ROWS, ROWS, 0)
    near_4 = away(half, 2)
    state = run_stage(FAR_12, state, far_12)
    near_3 = after(near_3, state)
    far_3 = other_core(near_3)
    state = run_stage(NEAR_3, state, near_3)
    near_4 = after(near_4, state)
    far_4 = other_core(near_4)
    state = run_stage(FAR_3_NEAR_4, state, jnp.concatenate([far_3, near_4], axis=0))
    return run_stage(FAR_4, state, far_4)


def solution(mesh):
    placed = P(("rep", "ctx"), "head")
    return jax.shard_map(
        per_device,
        mesh=mesh,
        in_specs=(placed, placed, placed, P("rep")),
        out_specs=placed,
        check_vma=False,
    )
```
